1024 devices in a mesh: dp: 128 (over x, y, z_hi, core), expert: 8 (over z_lo).
Axes of the slice: x: 4, y: 4, z: 32 (z_hi: 4, z_lo: 8; z = z_hi * 8 + z_lo), core: 2. Of those that a mesh axis runs over, the one named last changes fastest.
Arguments:
- d_out: bfloat16 [131072, 2048], P(('dp', 'expert')), may hold values from -0.09375 to 0.09375
- router_weight: float32 [131072, 2], P(('dp', 'expert')), may hold values from 0.05 to 0.95
- routes: int32 [131072, 2], P(('dp', 'expert')), may hold values from 0 to 15, all different within a row; in each aligned block of 128 rows (0 to 127, 128 to 255, ...) at most 32 rows name the same one
- gate_pre: bfloat16 [32768, 7168], P('dp'), may hold values from -6 to 6
- up_pre: bfloat16 [32768, 7168], P('dp'), may hold values from -24 to 24
Outputs:
- grad_down: float32 [7168, 2048], P('dp', 'expert')
The draws below stay inside these ranges and needn't reach their ends.
Inputs may be any that keep to these rules, and one draw needn't show every extreme that they name: `routes`: each row names two different experts. In each aligned block of 128 rows (one device's tokens) no expert is named by more than 32 rows, a bound that some block reaches.
All inputs are finite; a program needn't handle non-finite values.
Results may differ from the reference program's by a relative error of at most 0.004.
Values may be sent and summed in bfloat16 or wider, within the bound.
No kernel may reach another device: no remote copies, remote signals or barrier semaphores. Data moves between devices by JAX's collectives and lax.ppermute only.
A program may use at most 64 MiB of HBM per device.

```python
import math
import jax
import jax.numpy as jnp
import numpy as np
from jax import lax

D_WIN = 2048
FF_WIN = 7168
EXPERTS = 16
TOK_DEV = 128
CAP = 32
TOKENS = 131072
SLOTS_ALL = 32768
N_DP = 128
N_EXPERT = 8


def with_spikes(values, rng, source, target, parts, factor):
    owner, partner = [(jnp.arange(values.shape[dim]) // (values.shape[dim] // parts)).reshape([-1 if axis == dim else 1 for axis in range(values.ndim)]) for dim in (source, target)]
    chosen = jax.random.permutation(rng, parts)[partner]
    strong = (owner == chosen) | (owner == (partner + parts // 2) % parts)
    return jnp.where(strong, factor * values, values)


def block_scale(own_key, shape, split, least, high):
    def one(dim, parts):
        heights = jax.random.uniform(jax.random.fold_in(jax.random.fold_in(own_key, 6), dim), (parts,), jnp.float32, least / len(split), high / len(split))
        return jnp.repeat(jnp.exp(heights), shape[dim] // parts).reshape((-1,) + (1,) * (len(shape) - dim - 1))

    factor_of = one(*split[0])
    for cut in split[1:]:
        factor_of = factor_of * one(*cut)
    return factor_of


def assign_block(stream_key, own, number, rows, amount, top, limit, slope):
    order = jax.random.permutation(stream_key, amount)
    crowded, common = load_shares(amount, rows * top, limit, slope, True), load_shares(amount, rows * top, limit, slope, False)
    places = jnp.arange(amount)

    def named(lengths, turn):
        used = int((lengths > 0).sum())
        fixed = max(1, used // 4)
        moved = fixed + (places - fixed + turn * (used - fixed)) % max(1, amount - fixed)
        return jnp.zeros((amount,), jnp.int32).at[order[jnp.where(places < fixed, places, moved)]].set(jnp.asarray(lengths, jnp.int32))

    lengths = jnp.where(number % 4 == 0, named(crowded, number // 4), named(common, number - number // 4 - 1))
    mixed = jax.random.permutation(jax.random.fold_in(own, 3), amount)
    giver, taker = mixed[0:amount // 2 * 2:2], mixed[1:amount // 2 * 2:2]
    margin = jnp.minimum(lengths[giver] - 1, limit - lengths[taker]) // 2
    margin = jnp.where((giver == order[0]) | (taker == order[0]) | (lengths[taker] == 0), 0, jnp.maximum(margin, 0))
    moved = jax.random.randint(jax.random.fold_in(own, 4), (amount // 2,), 0, 1 << 20) % (margin + 1)
    lengths = lengths.at[giver].add(-moved).at[taker].add(moved)
    labels = jnp.searchsorted(jnp.cumsum(lengths), jnp.arange(rows * top), side="right").astype(jnp.int32)
    table = labels.reshape(top, rows).T
    table = table[jax.random.permutation(jax.random.fold_in(own, 1), rows)]
    turn = jax.random.randint(jax.random.fold_in(own, 2), (rows, 1), 0, top)
    return jnp.take_along_axis(table, (jnp.arange(top)[None, :] + turn) % top, axis=1)


def load_shares(amount, total, limit, lean, full):
    weights = [(1 << 20) // math.isqrt(rank ** lean) + 1 for rank in range(1, amount + 1)]
    largest = limit if full else min(limit, max(-(-total // amount), total * weights[0] // sum(weights)))
    least = 1 if total - largest >= amount - 1 else 0
    counts, surplus = [largest] + [least] * (amount - 1), total - largest - least * (amount - 1)
    while surplus > 0:
        candidates = [i for i in range(1, amount) if counts[i] < largest] or [i for i in range(1, amount) if counts[i] < limit]
        pool, left = sum([weights[i] for i in candidates]), surplus
        for i in candidates:
            addition = min(limit - counts[i], max(1, left * weights[i] // pool), surplus)
            counts[i] = counts[i] + addition
            surplus = surplus - addition
    return np.array(counts)


def centred(stream_key, dims, spread, most, split=(), held_as=jnp.bfloat16):
    array = jax.random.normal(stream_key, dims, jnp.float32) * spread
    if len(split) > 0:
        array = block_scale(stream_key, dims, split, -0.22, 0.18) * array
    return jnp.clip(array, min=-most, max=most).astype(held_as)


def bell_draw_with(key, extent, deviation, most, pieces, heavy, kind=jnp.bfloat16):
    result = deviation * jax.random.normal(key, extent, jnp.float32)
    if pieces:
        result = result * block_scale(key, extent, pieces, -0.22, 0.18)
    return jnp.clip(with_spikes(result, jax.random.fold_in(key, 3), *heavy), -most, most).astype(kind)


def setup_inputs(seed: int = 0) -> dict:
    key_list = jax.random.split(jax.random.key(seed), 6)
    d_out = centred(key_list[0], (TOKENS, D_WIN), (2.0 / (N_DP * N_EXPERT * 2 * TOK_DEV / EXPERTS) ** 0.5), 0.09375, ((0, 1024),))
    router_weight = jnp.clip(0.05 + 0.9 * jax.random.uniform(key_list[1], (TOKENS, 2), jnp.float32) ** block_scale(key_list[1], (TOKENS, 2), ((0, 1024),), -0.2, 0.2), 0.05, 0.95)
    routes_keys = jax.random.split(jax.random.fold_in(key_list[2], 1), TOKENS // TOK_DEV)
    routes_turns = jax.random.permutation(jax.random.fold_in(key_list[2], 3), TOKENS // TOK_DEV)
    routes = jax.vmap(lambda own, number: assign_block(jax.random.fold_in(key_list[2], 2), own, number, TOK_DEV, EXPERTS, 2, CAP, 1))(routes_keys, routes_turns).reshape((TOKENS, 2))
    gate_pre = centred(key_list[3], (SLOTS_ALL, FF_WIN), 1.0, 6.0, ((0, 128),))
    up_pre = bell_draw_with(key_list[4], (SLOTS_ALL, FF_WIN), 1.0, 24.0, ((0, 128),), (0, 1, 128, 5.5))
    return {"d_out": d_out, "router_weight": router_weight, "routes": routes, "gate_pre": gate_pre, "up_pre": up_pre}


def reference(d_out, router_weight, routes, gate_pre, up_pre):
    group_tokens = N_EXPERT * TOK_DEV
    slot_count = N_EXPERT * CAP

    def per_group(running, group_index):
        tokens = lax.dynamic_slice_in_dim(d_out, group_index * group_tokens, group_tokens, 0)
        weights = lax.dynamic_slice_in_dim(router_weight, group_index * group_tokens, group_tokens, 0)
        chosen = lax.dynamic_slice_in_dim(routes, group_index * group_tokens, group_tokens, 0)
        cotangent = (tokens.astype(jnp.float32)[:, None, :] * weights[:, :, None]).astype(jnp.bfloat16)
        cotangent = cotangent.reshape(2 * group_tokens, D_WIN)
        marked = (chosen.reshape(N_EXPERT, 2 * TOK_DEV) == 0).astype(jnp.int32)
        position = jnp.cumsum(marked, axis=1, dtype=jnp.int32) - marked
        source_rank = jnp.arange(N_EXPERT, dtype=jnp.int32)[:, None]
        slot_row = jnp.where(marked == 1, source_rank * CAP + position, slot_count).astype(jnp.int32)
        filled = jnp.zeros((slot_count, D_WIN), jnp.bfloat16)
        filled = filled.at[slot_row.reshape(-1)].set(cotangent, mode="drop")
        gate_rows = lax.dynamic_slice_in_dim(gate_pre, group_index * slot_count, slot_count, 0)
        up_rows = lax.dynamic_slice_in_dim(up_pre, group_index * slot_count, slot_count, 0)
        hidden = (jax.nn.silu(gate_rows.astype(jnp.float32)) * up_rows.astype(jnp.float32)).astype(jnp.bfloat16)
        partial_value = jnp.dot(hidden.T, filled, preferred_element_type=jnp.float32)
        return running + partial_value, None

    start_value = jnp.zeros((FF_WIN, D_WIN), jnp.float32)
    running, _ = lax.scan(per_group, start_value, jnp.arange(N_DP, dtype=jnp.int32))
    return running
```

```python
import jax
import jax.numpy as jnp
from jax import lax
from jax.sharding import Mesh, PartitionSpec as P

GRID = (("x", 4), ("y", 4), ("far", 4), ("core", 2))
SWAP = [(0, 1), (1, 0)]


def body(d_out, router_weight, routes, gate_pre, up_pre):
    group_count = lax.axis_size("expert")
    capacity = gate_pre.shape[0] // group_count
    planes = lax.axis_size("x") * lax.axis_size("y")
    fars = lax.axis_size("far")
    rows, units = gate_pre.shape
    width = d_out.shape[1] // group_count
    block = units // (planes * fars * 2)
    core = lax.axis_index("core")
    far = lax.axis_index("far")

    hidden = (jax.nn.silu(gate_pre.astype(jnp.float32)) * up_pre.astype(jnp.float32)).astype(
        jnp.bfloat16
    )
    turned = hidden.T.reshape(planes * fars, 2, block, rows)
    mine = lax.dynamic_index_in_dim(turned, core, 1, False).reshape(-1, rows)
    theirs = lax.dynamic_index_in_dim(turned, 1 - core, 1, False).reshape(-1, rows)
    met = lax.ppermute(theirs, "core", SWAP)

    named = routes == 0
    marked = jnp.any(named, axis=1)
    weight = jnp.sum(jnp.where(named, router_weight, 0.0), axis=1)
    count = marked.astype(jnp.int32)
    position = jnp.cumsum(count, dtype=jnp.int32) - count
    slots = lax.broadcasted_iota(jnp.int32, (capacity, d_out.shape[0]), 0)
    chosen = ((slots == position[None, :]) & marked[None, :]).astype(jnp.bfloat16)
    scaled = (d_out.astype(jnp.float32) * weight[:, None]).astype(jnp.bfloat16)
    outgoing = jnp.dot(chosen, scaled, preferred_element_type=jnp.float32).astype(jnp.bfloat16)
    incoming = lax.all_to_all(outgoing, "expert", split_axis=1, concat_axis=0, tiled=True)
    incoming_met = lax.ppermute(incoming, "core", SWAP)

    partial = jnp.dot(mine, incoming, preferred_element_type=jnp.float32) + jnp.dot(
        met, incoming_met, preferred_element_type=jnp.float32
    )
    partial = partial.astype(jnp.bfloat16).reshape(planes, fars * block, width)
    partial = lax.all_to_all(partial, ("x", "y"), split_axis=0, concat_axis=0, tiled=True)
    partial = jnp.sum(partial.astype(jnp.float32), axis=0).reshape(fars, block, width)
    result = lax.dynamic_index_in_dim(partial, far, 0, False)
    for step in range(1, fars):
        piece = lax.dynamic_index_in_dim(partial, (far + step) % fars, 0, False)
        piece = piece.astype(jnp.bfloat16)
        piece = lax.ppermute(piece, "far", [(i, (i + step) % fars) for i in range(fars)])
        result = result + piece.astype(jnp.float32)
    return result


def solution(mesh):
    names = tuple(name for name, _ in GRID)
    sizes = tuple(size for _, size in GRID)
    fine = Mesh(mesh.devices.reshape(sizes + (mesh.shape["expert"],)), names + ("expert",))
    tokens = P(names + ("expert",), None)
    slots = P(names, None)
    return jax.shard_map(
        body,
        mesh=fine,
        in_specs=(tokens, tokens, tokens, slots, slots),
        out_specs=P(names, "expert"),
        check_vma=False,
    )
```

```python
import functools

import jax
import jax.numpy as jnp
from jax import lax
from jax.experimental import pallas as pl
from jax.experimental.pallas import tpu as pltpu
from jax.sharding import Mesh, PartitionSpec as P

GRID = (("x", 4), ("y", 4), ("far", 4), ("core", 2))
SWAP = [(0, 1), (1, 0)]
PARTS = 8


def hidden_kernel(block, core_ref, gate_ref, up_ref, mine_ref, theirs_ref, gate, up, sems):
    parts, rows, part = gate.shape

    def copies(index):
        columns = pl.ds(index * part, part)
        return (
            pltpu.make_async_copy(gate_ref.at[:, columns], gate.at[index], sems.at[0, index]),
            pltpu.make_async_copy(up_ref.at[:, columns], up.at[index], sems.at[1, index]),
        )

    for index in range(parts):
        for copy in copies(index):
            copy.start()
    core = core_ref[0]
    for index in range(parts):
        for copy in copies(index):
            copy.wait()
        value = gate[index].astype(jnp.float32)
        value = value * (0.5 * jnp.tanh(0.5 * value) + 0.5) * up[index].astype(jnp.float32)
        value = value.astype(jnp.bfloat16).astype(jnp.float32)
        value = value.T.reshape(part // (2 * block), 2, block, rows)
        first = value[:, 0].reshape(part // 2, rows).astype(jnp.bfloat16)
        second = value[:, 1].reshape(part // 2, rows).astype(jnp.bfloat16)
        where = slice(index * (part // 2), (index + 1) * (part // 2))

        @pl.when(core == 0)
        def _():
            mine_ref[where, :] = first
            theirs_ref[where, :] = second

        @pl.when(core != 0)
        def _():
            mine_ref[where, :] = second
            theirs_ref[where, :] = first


def hidden_halves(core, gate_pre, up_pre, block):
    rows, units = gate_pre.shape
    half = jax.ShapeDtypeStruct((units // 2, rows), jnp.bfloat16)
    buffer = pltpu.VMEM((PARTS, rows, units // PARTS), jnp.bfloat16)
    return pl.pallas_call(
        functools.partial(hidden_kernel, block),
        in_specs=[
            pl.BlockSpec(memory_space=pltpu.SMEM),
            pl.BlockSpec(memory_space=pl.ANY),
            pl.BlockSpec(memory_space=pl.ANY),
        ],
        out_specs=[pl.BlockSpec(memory_space=pltpu.VMEM)] * 2,
        out_shape=[half, half],
        scratch_shapes=[buffer, buffer, pltpu.SemaphoreType.DMA((2, PARTS))],
        compiler_params=pltpu.CompilerParams(vmem_limit_bytes=52 << 20),
        cost_estimate=pl.CostEstimate(
            flops=8 * rows * units, bytes_accessed=6 * rows * units, transcendentals=rows * units
        ),
        name="hidden",
    )(core.reshape(1), gate_pre, up_pre)


def sum_kernel(terms_ref, sum_ref):
    total = terms_ref[0].astype(jnp.float32)
    for index in range(1, terms_ref.shape[0]):
        total = total + terms_ref[index].astype(jnp.float32)
    sum_ref[...] = total.astype(jnp.bfloat16)


def summed(terms):
    return pl.pallas_call(
        sum_kernel,
        in_specs=[pl.BlockSpec(memory_space=pltpu.VMEM)],
        out_specs=pl.BlockSpec(memory_space=pltpu.VMEM),
        out_shape=jax.ShapeDtypeStruct(terms.shape[1:], jnp.bfloat16),
        compiler_params=pltpu.CompilerParams(vmem_limit_bytes=16 << 20),
        name="plane_sum",
    )(terms)


def body(d_out, router_weight, routes, gate_pre, up_pre):
    group_count = lax.axis_size("expert")
    capacity = gate_pre.shape[0] // group_count
    planes = lax.axis_size("x") * lax.axis_size("y")
    fars = lax.axis_size("far")
    rows, units = gate_pre.shape
    width = d_out.shape[1] // group_count
    block = units // (planes * fars * 2)
    core = lax.axis_index("core")

    mine, theirs = hidden_halves(core, gate_pre, up_pre, block)
    met = lax.ppermute(theirs, "core", SWAP)

    named = routes == 0
    marked = jnp.any(named, axis=1)
    weight = jnp.sum(jnp.where(named, router_weight, 0.0), axis=1)
    count = marked.astype(jnp.int32)
    position = jnp.cumsum(count, dtype=jnp.int32) - count
    slots = lax.broadcasted_iota(jnp.int32, (capacity, d_out.shape[0]), 0)
    chosen = ((slots == position[None, :]) & marked[None, :]).astype(jnp.bfloat16)
    scaled = (d_out.astype(jnp.float32) * weight[:, None]).astype(jnp.bfloat16)
    outgoing = jnp.dot(chosen, scaled, preferred_element_type=jnp.float32).astype(jnp.bfloat16)
    incoming = lax.all_to_all(outgoing, "expert", split_axis=1, concat_axis=0, tiled=True)
    incoming_met = lax.ppermute(incoming, "core", SWAP)

    partial = jnp.dot(mine, incoming, preferred_element_type=jnp.float32) + jnp.dot(
        met, incoming_met, preferred_element_type=jnp.float32
    )
    partial = partial.astype(jnp.bfloat16).reshape(planes, fars * block, width)
    partial = lax.all_to_all(partial, ("x", "y"), split_axis=0, concat_axis=0, tiled=True)
    partial = summed(partial).reshape(fars, block, width)
    partial = lax.all_to_all(partial, "far", split_axis=0, concat_axis=0, tiled=True)
    return jnp.sum(partial.astype(jnp.float32), axis=0)


def solution(mesh):
    names = tuple(name for name, _ in GRID)
    sizes = tuple(size for _, size in GRID)
    fine = Mesh(mesh.devices.reshape(sizes + (mesh.shape["expert"],)), names + ("expert",))
    tokens = P(names + ("expert",), None)
    slots = P(names, None)
    return jax.shard_map(
        body,
        mesh=fine,
        in_specs=(tokens, tokens, tokens, slots, slots),
        out_specs=P(names, "expert"),
        check_vma=False,
    )
```

```python
import functools

import jax
import jax.numpy as jnp
from jax import lax
from jax.experimental import pallas as pl
from jax.experimental.pallas import tpu as pltpu
from jax.sharding import Mesh, PartitionSpec as P

GRID = (("x", 4), ("y", 4), ("far", 4), ("core", 2))
SWAP = [(0, 1), (1, 0)]
PARTS = 8


def hidden_kernel(block, core_ref, gate_ref, up_ref, mine_ref, theirs_ref, gate, up, sems):
    parts, rows, part = gate.shape

    def copies(index):
        columns = pl.ds(index * part, part)
        return (
            pltpu.make_async_copy(gate_ref.at[:, columns], gate.at[index], sems.at[0, index]),
            pltpu.make_async_copy(up_ref.at[:, columns], up.at[index], sems.at[1, index]),
        )

    for index in range(parts):
        for copy in copies(index):
            copy.start()
    core = core_ref[0]
    for index in range(parts):
        for copy in copies(index):
            copy.wait()
        value = gate[index].astype(jnp.float32)
        value = value * (0.5 * jnp.tanh(0.5 * value) + 0.5) * up[index].astype(jnp.float32)
        value = value.astype(jnp.bfloat16).astype(jnp.float32)
        value = value.T.reshape(part // (2 * block), 2, block, rows)
        first = value[:, 0].reshape(part // 2, rows).astype(jnp.bfloat16)
        second = value[:, 1].reshape(part // 2, rows).astype(jnp.bfloat16)
        where = slice(index * (part // 2), (index + 1) * (part // 2))

        @pl.when(core == 0)
        def _():
            mine_ref[where, :] = first
            theirs_ref[where, :] = second

        @pl.when(core != 0)
        def _():
            mine_ref[where, :] = second
            theirs_ref[where, :] = first


def hidden_halves(core, gate_pre, up_pre, block):
    rows, units = gate_pre.shape
    half = jax.ShapeDtypeStruct((units // 2, rows), jnp.bfloat16)
    buffer = pltpu.VMEM((PARTS, rows, units // PARTS), jnp.bfloat16)
    return pl.pallas_call(
        functools.partial(hidden_kernel, block),
        in_specs=[
            pl.BlockSpec(memory_space=pltpu.SMEM),
            pl.BlockSpec(memory_space=pl.ANY),
            pl.BlockSpec(memory_space=pl.ANY),
        ],
        out_specs=[pl.BlockSpec(memory_space=pltpu.VMEM)] * 2,
        out_shape=[half, half],
        scratch_shapes=[buffer, buffer, pltpu.SemaphoreType.DMA((2, PARTS))],
        compiler_params=pltpu.CompilerParams(vmem_limit_bytes=52 << 20),
        cost_estimate=pl.CostEstimate(
            flops=8 * rows * units, bytes_accessed=6 * rows * units, transcendentals=rows * units
        ),
        name="hidden",
    )(core.reshape(1), gate_pre, up_pre)


def routed_kernel(tokens_ref, weight_ref, routes_ref, outgoing_ref):
    groups, capacity, width = outgoing_ref.shape
    count = tokens_ref.shape[0]
    named = routes_ref[...] == 0
    marked = jnp.max(named.astype(jnp.float32), axis=0, keepdims=True)
    weight = jnp.sum(jnp.where(named, weight_ref[...], 0.0), axis=0, keepdims=True)
    earlier = lax.broadcasted_iota(jnp.int32, (count, count), 0)
    later = lax.broadcasted_iota(jnp.int32, (count, count), 1)
    before = (earlier < later).astype(jnp.bfloat16)
    position = jnp.dot(
        jnp.broadcast_to(marked, (8, count)).astype(jnp.bfloat16),
        before,
        preferred_element_type=jnp.float32,
    )[:1]
    slots = lax.broadcasted_iota(jnp.int32, (capacity, count), 0)
    taken = (slots == position.astype(jnp.int32)) & (marked > 0.5)
    chosen = taken.astype(jnp.bfloat16)
    scale = jnp.sum(jnp.where(taken, weight, 0.0), axis=1, keepdims=True)
    picked = jnp.dot(chosen, tokens_ref[...], preferred_element_type=jnp.float32)
    picked = (picked * scale).astype(jnp.bfloat16)
    for group in range(groups):
        outgoing_ref[group] = picked[:, group * width : (group + 1) * width]


def routed(tokens, weight, routes, groups, capacity):
    width = tokens.shape[1] // groups
    return pl.pallas_call(
        routed_kernel,
        in_specs=[pl.BlockSpec(memory_space=pltpu.VMEM)] * 3,
        out_specs=pl.BlockSpec(memory_space=pltpu.VMEM),
        out_shape=jax.ShapeDtypeStruct((groups, capacity, width), jnp.bfloat16),
        compiler_params=pltpu.CompilerParams(vmem_limit_bytes=16 << 20),
        name="routed",
    )(tokens, weight.T, routes.T)


def sum_kernel(terms_ref, sum_ref):
    total = terms_ref[0].astype(jnp.float32)
    for index in range(1, terms_ref.shape[0]):
        total = total + terms_ref[index].astype(jnp.float32)
    sum_ref[...] = total.astype(jnp.bfloat16)


def summed(terms):
    return pl.pallas_call(
        sum_kernel,
        in_specs=[pl.BlockSpec(memory_space=pltpu.VMEM)],
        out_specs=pl.BlockSpec(memory_space=pltpu.VMEM),
        out_shape=jax.ShapeDtypeStruct(terms.shape[1:], jnp.bfloat16),
        compiler_params=pltpu.CompilerParams(vmem_limit_bytes=16 << 20),
        name="plane_sum",
    )(terms)


def body(d_out, router_weight, routes, gate_pre, up_pre):
    group_count = lax.axis_size("expert")
    capacity = gate_pre.shape[0] // group_count
    planes = lax.axis_size("x") * lax.axis_size("y")
    fars = lax.axis_size("far")
    rows, units = gate_pre.shape
    width = d_out.shape[1] // group_count
    block = units // (planes * fars * 2)
    core = lax.axis_index("core")

    outgoing = routed(d_out, router_weight, routes, group_count, capacity)
    core, outgoing = lax.optimization_barrier((core, outgoing))
    mine, theirs = hidden_halves(core, gate_pre, up_pre, block)
    incoming = lax.all_to_all(outgoing, "expert", split_axis=0, concat_axis=0, tiled=True)
    incoming = incoming.reshape(rows, width)
    theirs, incoming = lax.optimization_barrier((theirs, incoming))
    met = lax.ppermute(theirs, "core", SWAP)
    incoming_met = lax.ppermute(incoming, "core", SWAP)

    partial = jnp.dot(mine, incoming, preferred_element_type=jnp.float32) + jnp.dot(
        met, incoming_met, preferred_element_type=jnp.float32
    )
    partial = partial.astype(jnp.bfloat16).reshape(planes, fars * block, width)
    partial = lax.all_to_all(partial, ("x", "y"), split_axis=0, concat_axis=0, tiled=True)
    partial = summed(partial).reshape(fars, block, width)
    partial = lax.all_to_all(partial, "far", split_axis=0, concat_axis=0, tiled=True)
    return jnp.sum(partial.astype(jnp.float32), axis=0)


def solution(mesh):
    names = tuple(name for name, _ in GRID)
    sizes = tuple(size for _, size in GRID)
    fine = Mesh(mesh.devices.reshape(sizes + (mesh.shape["expert"],)), names + ("expert",))
    tokens = P(names + ("expert",), None)
    slots = P(names, None)
    return jax.shard_map(
        body,
        mesh=fine,
        in_specs=(tokens, tokens, tokens, slots, slots),
        out_specs=P(names, "expert"),
        check_vma=False,
    )
```

```python
import functools

import jax
import jax.numpy as jnp
from jax import lax
from jax.experimental import pallas as pl
from jax.experimental.pallas import tpu as pltpu
from jax.sharding import Mesh, PartitionSpec as P

GRID = (("x", 4), ("y", 4), ("far", 4), ("core", 2))
SWAP = [(0, 1), (1, 0)]
PARTS = 8


def hidden_kernel(block, core_ref, gate_ref, up_ref, mine_ref, theirs_ref, gate, up, sems):
    parts, rows, part = gate.shape

    def copies(index):
        columns = pl.ds(index * part, part)
        return (
            pltpu.make_async_copy(gate_ref.at[:, columns], gate.at[index], sems.at[0, index]),
            pltpu.make_async_copy(up_ref.at[:, columns], up.at[index], sems.at[1, index]),
        )

    for index in range(parts):
        for copy in copies(index):
            copy.start()
    core = core_ref[0]
    for index in range(parts):
        for copy in copies(index):
            copy.wait()
        value = gate[index].astype(jnp.float32)
        value = value * (0.5 * jnp.tanh(0.5 * value) + 0.5) * up[index].astype(jnp.float32)
        value = value.astype(jnp.bfloat16).astype(jnp.float32)
        value = value.T.reshape(part // (2 * block), 2, block, rows)
        first = value[:, 0].reshape(part // 2, rows).astype(jnp.bfloat16)
        second = value[:, 1].reshape(part // 2, rows).astype(jnp.bfloat16)
        where = slice(index * (part // 2), (index + 1) * (part // 2))

        @pl.when(core == 0)
        def _():
            mine_ref[where, :] = first
            theirs_ref[where, :] = second

        @pl.when(core != 0)
        def _():
            mine_ref[where, :] = second
            theirs_ref[where, :] = first


def hidden_halves(core, gate_pre, up_pre, block):
    rows, units = gate_pre.shape
    half = jax.ShapeDtypeStruct((units // 2, rows), jnp.bfloat16)
    buffer = pltpu.VMEM((PARTS, rows, units // PARTS), jnp.bfloat16)
    return pl.pallas_call(
        functools.partial(hidden_kernel, block),
        in_specs=[
            pl.BlockSpec(memory_space=pltpu.SMEM),
            pl.BlockSpec(memory_space=pl.ANY),
            pl.BlockSpec(memory_space=pl.ANY),
        ],
        out_specs=[pl.BlockSpec(memory_space=pltpu.VMEM)] * 2,
        out_shape=[half, half],
        scratch_shapes=[buffer, buffer, pltpu.SemaphoreType.DMA((2, PARTS))],
        compiler_params=pltpu.CompilerParams(vmem_limit_bytes=52 << 20),
        cost_estimate=pl.CostEstimate(
            flops=8 * rows * units, bytes_accessed=6 * rows * units, transcendentals=rows * units
        ),
        name="hidden",
    )(core.reshape(1), gate_pre, up_pre)


def routed_kernel(tokens_from, weight_from, routes_from, outgoing_ref, *scratch):
    tokens_ref, weight_ref, routes_ref, sems = scratch
    copies = [
        pltpu.make_async_copy(source, target, sems.at[index])
        for index, (source, target) in enumerate(
            (
                (tokens_from, tokens_ref),
                (weight_from, weight_ref),
                (routes_from, routes_ref),
            )
        )
    ]
    for copy in copies:
        copy.start()
    groups, capacity, width = outgoing_ref.shape
    count = tokens_ref.shape[0]
    copies[2].wait()
    copies[1].wait()
    named = routes_ref[...] == 0
    marked = jnp.max(named.astype(jnp.float32), axis=0, keepdims=True)
    weight = jnp.sum(jnp.where(named, weight_ref[...], 0.0), axis=0, keepdims=True)
    earlier = lax.broadcasted_iota(jnp.int32, (count, count), 0)
    later = lax.broadcasted_iota(jnp.int32, (count, count), 1)
    before = (earlier < later).astype(jnp.bfloat16)
    position = jnp.dot(
        jnp.broadcast_to(marked, (8, count)).astype(jnp.bfloat16),
        before,
        preferred_element_type=jnp.float32,
    )[:1]
    slots = lax.broadcasted_iota(jnp.int32, (capacity, count), 0)
    taken = (slots == position.astype(jnp.int32)) & (marked > 0.5)
    chosen = taken.astype(jnp.bfloat16)
    scale = jnp.sum(jnp.where(taken, weight, 0.0), axis=1, keepdims=True)
    copies[0].wait()
    picked = jnp.dot(chosen, tokens_ref[...], preferred_element_type=jnp.float32)
    picked = (picked * scale).astype(jnp.bfloat16)
    for group in range(groups):
        outgoing_ref[group] = picked[:, group * width : (group + 1) * width]


def routed(tokens, weight, routes, groups, capacity):
    width = tokens.shape[1] // groups
    return pl.pallas_call(
        routed_kernel,
        in_specs=[pl.BlockSpec(memory_space=pl.ANY)] * 3,
        out_specs=pl.BlockSpec(memory_space=pltpu.VMEM),
        out_shape=jax.ShapeDtypeStruct((groups, capacity, width), jnp.bfloat16),
        scratch_shapes=[
            pltpu.VMEM(tokens.shape, tokens.dtype),
            pltpu.VMEM(weight.shape[::-1], weight.dtype),
            pltpu.VMEM(routes.shape[::-1], routes.dtype),
            pltpu.SemaphoreType.DMA((3,)),
        ],
        compiler_params=pltpu.CompilerParams(vmem_limit_bytes=62 << 20),
        name="routed",
    )(tokens, weight.T, routes.T)


def sum_kernel(order_ref, terms_ref, own_ref, passed_ref, sent_ref, total_ref):
    total = terms_ref[0].astype(jnp.float32)
    for index in range(1, terms_ref.shape[0]):
        total = total + terms_ref[index].astype(jnp.float32)
    total_ref[...] = total.reshape(total_ref.shape)
    own_ref[...] = total_ref[order_ref[0]]
    passed_ref[...] = total_ref[order_ref[1]]
    sent = jnp.concatenate([total_ref[order_ref[2]], total_ref[order_ref[3]]], axis=0)
    sent_ref[...] = sent.astype(jnp.bfloat16)


def summed(order, terms, fars):
    block, width = terms.shape[1] // fars, terms.shape[2]
    piece = jax.ShapeDtypeStruct((block, width), jnp.float32)
    return pl.pallas_call(
        sum_kernel,
        in_specs=[
            pl.BlockSpec(memory_space=pltpu.SMEM),
            pl.BlockSpec(memory_space=pltpu.VMEM),
        ],
        out_specs=[pl.BlockSpec(memory_space=pltpu.VMEM)] * 3,
        out_shape=[piece, piece, jax.ShapeDtypeStruct((2 * block, width), jnp.bfloat16)],
        scratch_shapes=[pltpu.VMEM((fars, block, width), jnp.float32)],
        compiler_params=pltpu.CompilerParams(vmem_limit_bytes=16 << 20),
        name="plane_sum",
    )(order, terms)


def body(d_out, router_weight, routes, gate_pre, up_pre):
    group_count = lax.axis_size("expert")
    capacity = gate_pre.shape[0] // group_count
    planes = lax.axis_size("x") * lax.axis_size("y")
    fars = lax.axis_size("far")
    rows, units = gate_pre.shape
    width = d_out.shape[1] // group_count
    block = units // (planes * fars * 2)
    core = lax.axis_index("core")

    outgoing = routed(d_out, router_weight, routes, group_count, capacity)
    far = lax.axis_index("far")
    order = jnp.stack([far, far ^ 3, far ^ 1, far ^ 2])
    core, order, outgoing = lax.optimization_barrier((core, order, outgoing))
    mine, theirs = hidden_halves(core, gate_pre, up_pre, block)
    incoming = lax.all_to_all(outgoing, "expert", split_axis=0, concat_axis=0, tiled=True)
    incoming = incoming.reshape(rows, width)
    theirs, incoming = lax.optimization_barrier((theirs, incoming))
    met = lax.ppermute(theirs, "core", SWAP)
    incoming_met = lax.ppermute(incoming, "core", SWAP)

    partial = jnp.dot(mine, incoming, preferred_element_type=jnp.float32) + jnp.dot(
        met, incoming_met, preferred_element_type=jnp.float32
    )
    partial = partial.astype(jnp.bfloat16).reshape(planes, fars * block, width)
    partial = lax.all_to_all(partial, ("x", "y"), split_axis=0, concat_axis=0, tiled=True)
    own, passed, sent = summed(order, partial, fars)
    sent = lax.ppermute(sent, "far", [(i, i ^ 1) for i in range(fars)]).astype(jnp.float32)
    passed = (passed + sent[block:]).astype(jnp.bfloat16)
    passed = lax.ppermute(passed, "far", [(i, i ^ 3) for i in range(fars)])
    return own + sent[:block] + passed.astype(jnp.float32)


def solution(mesh):
    names = tuple(name for name, _ in GRID)
    sizes = tuple(size for _, size in GRID)
    fine = Mesh(mesh.devices.reshape(sizes + (mesh.shape["expert"],)), names + ("expert",))
    tokens = P(names + ("expert",), None)
    slots = P(names, None)
    return jax.shard_map(
        body,
        mesh=fine,
        in_specs=(tokens, tokens, tokens, slots, slots),
        out_specs=P(names, "expert"),
        check_vma=False,
    )
```

```python
import functools

import jax
import jax.numpy as jnp
from jax import lax
from jax.experimental import pallas as pl
from jax.experimental.pallas import tpu as pltpu
from jax.sharding import Mesh, PartitionSpec as P

GRID = (("x", 4), ("y", 4), ("far", 4), ("core", 2))
SWAP = [(0, 1), (1, 0)]
PARTS = 8


def hidden_kernel(block, core_ref, gate_ref, up_ref, mine_ref, theirs_ref, gate, up, sems):
    parts, rows, part = gate.shape

    def copies(index):
        columns = pl.ds(index * part, part)
        return (
            pltpu.make_async_copy(gate_ref.at[:, columns], gate.at[index], sems.at[0, index]),
            pltpu.make_async_copy(up_ref.at[:, columns], up.at[index], sems.at[1, index]),
        )

    for index in range(parts):
        for copy in copies(index):
            copy.start()
    core = core_ref[0]
    for index in range(parts):
        for copy in copies(index):
            copy.wait()
        value = gate[index].astype(jnp.float32)
        value = value * (0.5 * jnp.tanh(0.5 * value) + 0.5) * up[index].astype(jnp.float32)
        value = value.astype(jnp.bfloat16).astype(jnp.float32)
        value = value.T.reshape(part // (2 * block), 2, block, rows)
        first = value[:, 0].reshape(part // 2, rows).astype(jnp.bfloat16)
        second = value[:, 1].reshape(part // 2, rows).astype(jnp.bfloat16)
        where = slice(index * (part // 2), (index + 1) * (part // 2))

        @pl.when(core == 0)
        def _():
            mine_ref[where, :] = first
            theirs_ref[where, :] = second

        @pl.when(core != 0)
        def _():
            mine_ref[where, :] = second
            theirs_ref[where, :] = first


def hidden_halves(core, gate_pre, up_pre, block):
    rows, units = gate_pre.shape
    half = jax.ShapeDtypeStruct((units // 2, rows), jnp.bfloat16)
    buffer = pltpu.VMEM((PARTS, rows, units // PARTS), jnp.bfloat16)
    return pl.pallas_call(
        functools.partial(hidden_kernel, block),
        in_specs=[
            pl.BlockSpec(memory_space=pltpu.SMEM),
            pl.BlockSpec(memory_space=pl.ANY),
            pl.BlockSpec(memory_space=pl.ANY),
        ],
        out_specs=[pl.BlockSpec(memory_space=pltpu.VMEM)] * 2,
        out_shape=[half, half],
        scratch_shapes=[buffer, buffer, pltpu.SemaphoreType.DMA((2, PARTS))],
        compiler_params=pltpu.CompilerParams(vmem_limit_bytes=52 << 20),
        cost_estimate=pl.CostEstimate(
            flops=8 * rows * units, bytes_accessed=6 * rows * units, transcendentals=rows * units
        ),
        name="hidden",
    )(core.reshape(1), gate_pre, up_pre)


def routed_kernel(tokens_from, weight_from, routes_from, outgoing_ref, *scratch):
    tokens_ref, weight_ref, routes_ref, sems = scratch
    copies = [
        pltpu.make_async_copy(source, target, sems.at[index])
        for index, (source, target) in enumerate(
            (
                (routes_from, routes_ref),
                (weight_from, weight_ref),
                (tokens_from, tokens_ref),
            )
        )
    ]
    for copy in copies:
        copy.start()
    groups, capacity, width = outgoing_ref.shape
    count = tokens_ref.shape[0]
    earlier = lax.broadcasted_iota(jnp.int32, (count, count), 0)
    later = lax.broadcasted_iota(jnp.int32, (count, count), 1)
    before = (earlier < later).astype(jnp.bfloat16)
    slots = lax.broadcasted_iota(jnp.int32, (capacity, count), 0)
    copies[0].wait()
    copies[1].wait()
    named = routes_ref[...] == 0
    marked = jnp.max(named.astype(jnp.float32), axis=0, keepdims=True)
    weight = jnp.sum(jnp.where(named, weight_ref[...], 0.0), axis=0, keepdims=True)
    position = jnp.dot(
        jnp.broadcast_to(marked, (8, count)).astype(jnp.bfloat16),
        before,
        preferred_element_type=jnp.float32,
    )[:1]
    taken = (slots == position.astype(jnp.int32)) & (marked > 0.5)
    chosen = taken.astype(jnp.bfloat16)
    scale = jnp.sum(jnp.where(taken, weight, 0.0), axis=1, keepdims=True)
    copies[2].wait()
    picked = jnp.dot(chosen, tokens_ref[...], preferred_element_type=jnp.float32)
    picked = (picked * scale).astype(jnp.bfloat16)
    for group in range(groups):
        outgoing_ref[group] = picked[:, group * width : (group + 1) * width]


def routed(tokens, weight, routes, groups, capacity):
    width = tokens.shape[1] // groups
    return pl.pallas_call(
        routed_kernel,
        in_specs=[pl.BlockSpec(memory_space=pl.ANY)] * 3,
        out_specs=pl.BlockSpec(memory_space=pltpu.VMEM),
        out_shape=jax.ShapeDtypeStruct((groups, capacity, width), jnp.bfloat16),
        scratch_shapes=[
            pltpu.VMEM(tokens.shape, tokens.dtype),
            pltpu.VMEM(weight.shape[::-1], weight.dtype),
            pltpu.VMEM(routes.shape[::-1], routes.dtype),
            pltpu.SemaphoreType.DMA((3,)),
        ],
        compiler_params=pltpu.CompilerParams(vmem_limit_bytes=62 << 20),
        name="routed",
    )(tokens, weight.T, routes.T)


def sum_kernel(far_ref, terms_ref, own_ref, passed_ref, sent_ref):
    block, width = own_ref.shape
    total = terms_ref[0].astype(jnp.float32)
    for index in range(1, terms_ref.shape[0]):
        total = total + terms_ref[index].astype(jnp.float32)
    total = total.reshape(-1, block, width)
    for far in range(total.shape[0]):

        @pl.when(far_ref[0] == far)
        def _():
            own_ref[...] = total[far]
            passed_ref[...] = total[far ^ 3]
            sent = jnp.concatenate([total[far ^ 1], total[far ^ 2]], axis=0)
            sent_ref[...] = sent.astype(jnp.bfloat16)


def summed(far, terms, fars):
    block, width = terms.shape[1] // fars, terms.shape[2]
    piece = jax.ShapeDtypeStruct((block, width), jnp.float32)
    return pl.pallas_call(
        sum_kernel,
        in_specs=[
            pl.BlockSpec(memory_space=pltpu.SMEM),
            pl.BlockSpec(memory_space=pltpu.VMEM),
        ],
        out_specs=[pl.BlockSpec(memory_space=pltpu.VMEM)] * 3,
        out_shape=[piece, piece, jax.ShapeDtypeStruct((2 * block, width), jnp.bfloat16)],
        compiler_params=pltpu.CompilerParams(vmem_limit_bytes=16 << 20),
        name="plane_sum",
    )(far.reshape(1), terms)


def body(d_out, router_weight, routes, gate_pre, up_pre):
    group_count = lax.axis_size("expert")
    capacity = gate_pre.shape[0] // group_count
    planes = lax.axis_size("x") * lax.axis_size("y")
    fars = lax.axis_size("far")
    rows, units = gate_pre.shape
    width = d_out.shape[1] // group_count
    block = units // (planes * fars * 2)
    core = lax.axis_index("core")

    outgoing = routed(d_out, router_weight, routes, group_count, capacity)
    far = lax.axis_index("far")
    core, far, outgoing = lax.optimization_barrier((core, far, outgoing))
    mine, theirs = hidden_halves(core, gate_pre, up_pre, block)
    incoming = lax.all_to_all(outgoing, "expert", split_axis=0, concat_axis=0, tiled=True)
    incoming = incoming.reshape(rows, width)
    theirs, incoming = lax.optimization_barrier((theirs, incoming))
    met = lax.ppermute(theirs, "core", SWAP)
    incoming_met = lax.ppermute(incoming, "core", SWAP)

    partial = jnp.dot(mine, incoming, preferred_element_type=jnp.float32) + jnp.dot(
        met, incoming_met, preferred_element_type=jnp.float32
    )
    partial = partial.astype(jnp.bfloat16).reshape(planes, fars * block, width)
    partial = lax.all_to_all(partial, ("x", "y"), split_axis=0, concat_axis=0, tiled=True)
    own, passed, sent = summed(far, partial, fars)
    sent = lax.ppermute(sent, "far", [(i, i ^ 1) for i in range(fars)]).astype(jnp.float32)
    passed = (passed + sent[block:]).astype(jnp.bfloat16)
    passed = lax.ppermute(passed, "far", [(i, i ^ 3) for i in range(fars)])
    return own + sent[:block] + passed.astype(jnp.float32)


def solution(mesh):
    names = tuple(name for name, _ in GRID)
    sizes = tuple(size for _, size in GRID)
    fine = Mesh(mesh.devices.reshape(sizes + (mesh.shape["expert"],)), names + ("expert",))
    tokens = P(names + ("expert",), None)
    slots = P(names, None)
    return jax.shard_map(
        body,
        mesh=fine,
        in_specs=(tokens, tokens, tokens, slots, slots),
        out_specs=P(names, "expert"),
        check_vma=False,
    )
```

```python
import functools
import itertools

import jax
import jax.numpy as jnp
from jax import lax
from jax.experimental import pallas as pl
from jax.experimental.pallas import tpu as pltpu
from jax.sharding import Mesh, PartitionSpec as P

GRID = (("x", 4), ("y", 4), ("far", 4), ("core", 2))
SWAP = [(0, 1), (1, 0)]
PARTS = 8
PARTNERS = ((1, 3), (3, 1))


def mirrored(step, fars):
    return [
        (2 * far + core, 2 * (far ^ PARTNERS[step][core]) + core)
        for far in range(fars)
        for core in (0, 1)
    ]


def hidden_kernel(block, core_ref, gate_ref, up_ref, mine_ref, theirs_ref, gate, up, sems):
    parts, rows, part = gate.shape

    def copies(index):
        columns = pl.ds(index * part, part)
        return (
            pltpu.make_async_copy(gate_ref.at[:, columns], gate.at[index], sems.at[0, index]),
            pltpu.make_async_copy(up_ref.at[:, columns], up.at[index], sems.at[1, index]),
        )

    for index in range(parts):
        for copy in copies(index):
            copy.start()
    core = core_ref[0]
    for index in range(parts):
        for copy in copies(index):
            copy.wait()
        value = gate[index].astype(jnp.float32)
        value = value * (0.5 * jnp.tanh(0.5 * value) + 0.5) * up[index].astype(jnp.float32)
        value = value.astype(jnp.bfloat16).astype(jnp.float32)
        value = value.T.reshape(part // (2 * block), 2, block, rows)
        first = value[:, 0].reshape(part // 2, rows).astype(jnp.bfloat16)
        second = value[:, 1].reshape(part // 2, rows).astype(jnp.bfloat16)
        where = slice(index * (part // 2), (index + 1) * (part // 2))

        @pl.when(core == 0)
        def _():
            mine_ref[where, :] = first
            theirs_ref[where, :] = second

        @pl.when(core != 0)
        def _():
            mine_ref[where, :] = second
            theirs_ref[where, :] = first


def hidden_halves(core, gate_pre, up_pre, block):
    rows, units = gate_pre.shape
    half = jax.ShapeDtypeStruct((units // 2, rows), jnp.bfloat16)
    buffer = pltpu.VMEM((PARTS, rows, units // PARTS), jnp.bfloat16)
    return pl.pallas_call(
        functools.partial(hidden_kernel, block),
        in_specs=[
            pl.BlockSpec(memory_space=pltpu.SMEM),
            pl.BlockSpec(memory_space=pl.ANY),
            pl.BlockSpec(memory_space=pl.ANY),
        ],
        out_specs=[pl.BlockSpec(memory_space=pltpu.VMEM)] * 2,
        out_shape=[half, half],
        scratch_shapes=[buffer, buffer, pltpu.SemaphoreType.DMA((2, PARTS))],
        compiler_params=pltpu.CompilerParams(vmem_limit_bytes=52 << 20),
        cost_estimate=pl.CostEstimate(
            flops=8 * rows * units, bytes_accessed=6 * rows * units, transcendentals=rows * units
        ),
        name="hidden",
    )(core.reshape(1), gate_pre, up_pre)


def routed_kernel(tokens_from, weight_from, routes_from, outgoing_ref, *scratch):
    tokens_ref, weight_ref, routes_ref, sems = scratch
    copies = [
        pltpu.make_async_copy(source, target, sems.at[index])
        for index, (source, target) in enumerate(
            (
                (routes_from, routes_ref),
                (weight_from, weight_ref),
                (tokens_from, tokens_ref),
            )
        )
    ]
    for copy in copies:
        copy.start()
    groups, capacity, width = outgoing_ref.shape
    count = tokens_ref.shape[0]
    earlier = lax.broadcasted_iota(jnp.int32, (count, count), 0)
    later = lax.broadcasted_iota(jnp.int32, (count, count), 1)
    before = (earlier < later).astype(jnp.bfloat16)
    slots = lax.broadcasted_iota(jnp.int32, (capacity, count), 0)
    copies[0].wait()
    copies[1].wait()
    named = routes_ref[...] == 0
    marked = jnp.max(named.astype(jnp.float32), axis=0, keepdims=True)
    weight = jnp.sum(jnp.where(named, weight_ref[...], 0.0), axis=0, keepdims=True)
    position = jnp.dot(
        jnp.broadcast_to(marked, (8, count)).astype(jnp.bfloat16),
        before,
        preferred_element_type=jnp.float32,
    )[:1]
    taken = (slots == position.astype(jnp.int32)) & (marked > 0.5)
    chosen = taken.astype(jnp.bfloat16)
    scale = jnp.sum(jnp.where(taken, weight, 0.0), axis=1, keepdims=True)
    copies[2].wait()
    picked = jnp.dot(chosen, tokens_ref[...], preferred_element_type=jnp.float32)
    picked = (picked * scale).astype(jnp.bfloat16)
    for group in range(groups):
        outgoing_ref[group] = picked[:, group * width : (group + 1) * width]


def routed(tokens, weight, routes, groups, capacity):
    width = tokens.shape[1] // groups
    return pl.pallas_call(
        routed_kernel,
        in_specs=[pl.BlockSpec(memory_space=pl.ANY)] * 3,
        out_specs=pl.BlockSpec(memory_space=pltpu.VMEM),
        out_shape=jax.ShapeDtypeStruct((groups, capacity, width), jnp.bfloat16),
        scratch_shapes=[
            pltpu.VMEM(tokens.shape, tokens.dtype),
            pltpu.VMEM(weight.shape[::-1], weight.dtype),
            pltpu.VMEM(routes.shape[::-1], routes.dtype),
            pltpu.SemaphoreType.DMA((3,)),
        ],
        compiler_params=pltpu.CompilerParams(vmem_limit_bytes=62 << 20),
        name="routed",
    )(tokens, weight.T, routes.T)


def sum_kernel(place_ref, terms_ref, own_ref, passed_ref, sent_ref):
    block, width = own_ref.shape
    total = terms_ref[0].astype(jnp.float32)
    for index in range(1, terms_ref.shape[0]):
        total = total + terms_ref[index].astype(jnp.float32)
    total = total.reshape(-1, block, width)
    for place, (far, core) in enumerate(itertools.product(range(total.shape[0]), (0, 1))):

        @pl.when(place_ref[0] == place)
        def _():
            own_ref[...] = total[far]
            passed_ref[...] = total[far ^ PARTNERS[1][core]]
            sent = jnp.concatenate([total[far ^ PARTNERS[0][core]], total[far ^ 2]], axis=0)
            sent_ref[...] = sent.astype(jnp.bfloat16)


def summed(place, terms, fars):
    block, width = terms.shape[1] // fars, terms.shape[2]
    piece = jax.ShapeDtypeStruct((block, width), jnp.float32)
    return pl.pallas_call(
        sum_kernel,
        in_specs=[
            pl.BlockSpec(memory_space=pltpu.SMEM),
            pl.BlockSpec(memory_space=pltpu.VMEM),
        ],
        out_specs=[pl.BlockSpec(memory_space=pltpu.VMEM)] * 3,
        out_shape=[piece, piece, jax.ShapeDtypeStruct((2 * block, width), jnp.bfloat16)],
        compiler_params=pltpu.CompilerParams(vmem_limit_bytes=16 << 20),
        name="plane_sum",
    )(place.reshape(1), terms)


def body(d_out, router_weight, routes, gate_pre, up_pre):
    group_count = lax.axis_size("expert")
    capacity = gate_pre.shape[0] // group_count
    planes = lax.axis_size("x") * lax.axis_size("y")
    fars = lax.axis_size("far")
    rows, units = gate_pre.shape
    width = d_out.shape[1] // group_count
    block = units // (planes * fars * 2)
    core = lax.axis_index("core")

    outgoing = routed(d_out, router_weight, routes, group_count, capacity)
    place = lax.axis_index(("far", "core"))
    core, place, outgoing = lax.optimization_barrier((core, place, outgoing))
    mine, theirs = hidden_halves(core, gate_pre, up_pre, block)
    incoming = lax.all_to_all(outgoing, "expert", split_axis=0, concat_axis=0, tiled=True)
    incoming = incoming.reshape(rows, width)
    theirs, incoming = lax.optimization_barrier((theirs, incoming))
    met = lax.ppermute(theirs, "core", SWAP)
    incoming_met = lax.ppermute(incoming, "core", SWAP)

    partial = jnp.dot(mine, incoming, preferred_element_type=jnp.float32) + jnp.dot(
        met, incoming_met, preferred_element_type=jnp.float32
    )
    partial = partial.astype(jnp.bfloat16).reshape(planes, fars * block, width)
    partial = lax.all_to_all(partial, ("x", "y"), split_axis=0, concat_axis=0, tiled=True)
    own, passed, sent = summed(place, partial, fars)
    sent = lax.ppermute(sent, ("far", "core"), mirrored(0, fars)).astype(jnp.float32)
    passed = (passed + sent[block:]).astype(jnp.bfloat16)
    passed = lax.ppermute(passed, ("far", "core"), mirrored(1, fars))
    return own + sent[:block] + passed.astype(jnp.float32)


def solution(mesh):
    names = tuple(name for name, _ in GRID)
    sizes = tuple(size for _, size in GRID)
    fine = Mesh(mesh.devices.reshape(sizes + (mesh.shape["expert"],)), names + ("expert",))
    tokens = P(names + ("expert",), None)
    slots = P(names, None)
    return jax.shard_map(
        body,
        mesh=fine,
        in_specs=(tokens, tokens, tokens, slots, slots),
        out_specs=P(names, "expert"),
        check_vma=False,
    )
```

```python
import functools
import itertools

import jax
import jax.numpy as jnp
from jax import lax
from jax.experimental import pallas as pl
from jax.experimental.pallas import tpu as pltpu
from jax.sharding import Mesh, PartitionSpec as P

GRID = (("x", 4), ("y", 4), ("far", 4), ("core", 2))
SWAP = [(0, 1), (1, 0)]
PARTS = 8
PARTNERS = ((3, 1), (1, 3))


def mirrored(step, fars):
    return [
        (2 * far + core, 2 * (far ^ PARTNERS[step][core]) + core)
        for far in range(fars)
        for core in (0, 1)
    ]


def hidden_kernel(block, core_ref, gate_ref, up_ref, mine_ref, theirs_ref, gate, up, sems):
    parts, rows, part = gate.shape

    def copies(index):
        columns = pl.ds(index * part, part)
        return (
            pltpu.make_async_copy(gate_ref.at[:, columns], gate.at[index], sems.at[0, index]),
            pltpu.make_async_copy(up_ref.at[:, columns], up.at[index], sems.at[1, index]),
        )

    for index in range(parts):
        for copy in copies(index):
            copy.start()
    core = core_ref[0]
    for index in range(parts):
        for copy in copies(index):
            copy.wait()
        value = gate[index].astype(jnp.float32)
        value = value * (0.5 * jnp.tanh(0.5 * value) + 0.5) * up[index].astype(jnp.float32)
        value = value.astype(jnp.bfloat16).astype(jnp.float32)
        value = value.T.reshape(part // (2 * block), 2, block, rows)
        first = value[:, 0].reshape(part // 2, rows).astype(jnp.bfloat16)
        second = value[:, 1].reshape(part // 2, rows).astype(jnp.bfloat16)
        where = slice(index * (part // 2), (index + 1) * (part // 2))

        @pl.when(core == 0)
        def _():
            mine_ref[where, :] = first
            theirs_ref[where, :] = second

        @pl.when(core != 0)
        def _():
            mine_ref[where, :] = second
            theirs_ref[where, :] = first


def hidden_halves(core, gate_pre, up_pre, block):
    rows, units = gate_pre.shape
    half = jax.ShapeDtypeStruct((units // 2, rows), jnp.bfloat16)
    buffer = pltpu.VMEM((PARTS, rows, units // PARTS), jnp.bfloat16)
    return pl.pallas_call(
        functools.partial(hidden_kernel, block),
        in_specs=[
            pl.BlockSpec(memory_space=pltpu.SMEM),
            pl.BlockSpec(memory_space=pl.ANY),
            pl.BlockSpec(memory_space=pl.ANY),
        ],
        out_specs=[pl.BlockSpec(memory_space=pltpu.VMEM)] * 2,
        out_shape=[half, half],
        scratch_shapes=[buffer, buffer, pltpu.SemaphoreType.DMA((2, PARTS))],
        compiler_params=pltpu.CompilerParams(vmem_limit_bytes=52 << 20),
        cost_estimate=pl.CostEstimate(
            flops=8 * rows * units, bytes_accessed=6 * rows * units, transcendentals=rows * units
        ),
        name="hidden",
    )(core.reshape(1), gate_pre, up_pre)


def routed_kernel(tokens_from, weight_from, routes_from, outgoing_ref, *scratch):
    tokens_ref, weight_ref, routes_ref, sems = scratch
    copies = [
        pltpu.make_async_copy(source, target, sems.at[index])
        for index, (source, target) in enumerate(
            (
                (routes_from, routes_ref),
                (weight_from, weight_ref),
                (tokens_from, tokens_ref),
            )
        )
    ]
    for copy in copies:
        copy.start()
    groups, capacity, width = outgoing_ref.shape
    count = tokens_ref.shape[0]
    earlier = lax.broadcasted_iota(jnp.int32, (count, count), 0)
    later = lax.broadcasted_iota(jnp.int32, (count, count), 1)
    before = (earlier < later).astype(jnp.bfloat16)
    slots = lax.broadcasted_iota(jnp.int32, (capacity, count), 0)
    copies[0].wait()
    copies[1].wait()
    named = routes_ref[...] == 0
    marked = jnp.max(named.astype(jnp.float32), axis=0, keepdims=True)
    weight = jnp.sum(jnp.where(named, weight_ref[...], 0.0), axis=0, keepdims=True)
    position = jnp.dot(
        jnp.broadcast_to(marked, (8, count)).astype(jnp.bfloat16),
        before,
        preferred_element_type=jnp.float32,
    )[:1]
    taken = (slots == position.astype(jnp.int32)) & (marked > 0.5)
    chosen = taken.astype(jnp.bfloat16)
    scale = jnp.sum(jnp.where(taken, weight, 0.0), axis=1, keepdims=True)
    copies[2].wait()
    picked = jnp.dot(chosen, tokens_ref[...], preferred_element_type=jnp.float32)
    picked = (picked * scale).astype(jnp.bfloat16)
    for group in range(groups):
        outgoing_ref[group] = picked[:, group * width : (group + 1) * width]


def routed(tokens, weight, routes, groups, capacity):
    width = tokens.shape[1] // groups
    return pl.pallas_call(
        routed_kernel,
        in_specs=[pl.BlockSpec(memory_space=pl.ANY)] * 3,
        out_specs=pl.BlockSpec(memory_space=pltpu.VMEM),
        out_shape=jax.ShapeDtypeStruct((groups, capacity, width), jnp.bfloat16),
        scratch_shapes=[
            pltpu.VMEM(tokens.shape, tokens.dtype),
            pltpu.VMEM(weight.shape[::-1], weight.dtype),
            pltpu.VMEM(routes.shape[::-1], routes.dtype),
            pltpu.SemaphoreType.DMA((3,)),
        ],
        compiler_params=pltpu.CompilerParams(vmem_limit_bytes=62 << 20),
        name="routed",
    )(tokens, weight.T, routes.T)


def sum_kernel(place_ref, terms_ref, own_ref, passed_ref, sent_ref):
    block, width = own_ref.shape
    total = terms_ref[0].astype(jnp.float32)
    for index in range(1, terms_ref.shape[0]):
        total = total + terms_ref[index].astype(jnp.float32)
    total = total.reshape(-1, block, width)
    for place, (far, core) in enumerate(itertools.product(range(total.shape[0]), (0, 1))):

        @pl.when(place_ref[0] == place)
        def _():
            own_ref[...] = total[far]
            passed_ref[...] = total[far ^ PARTNERS[1][core]]
            sent = jnp.concatenate([total[far ^ PARTNERS[0][core]], total[far ^ 2]], axis=0)
            sent_ref[...] = sent.astype(jnp.bfloat16)


def summed(place, terms, fars):
    block, width = terms.shape[1] // fars, terms.shape[2]
    piece = jax.ShapeDtypeStruct((block, width), jnp.float32)
    return pl.pallas_call(
        sum_kernel,
        in_specs=[
            pl.BlockSpec(memory_space=pltpu.SMEM),
            pl.BlockSpec(memory_space=pltpu.VMEM),
        ],
        out_specs=[pl.BlockSpec(memory_space=pltpu.VMEM)] * 3,
        out_shape=[piece, piece, jax.ShapeDtypeStruct((2 * block, width), jnp.bfloat16)],
        compiler_params=pltpu.CompilerParams(vmem_limit_bytes=16 << 20),
        name="plane_sum",
    )(place.reshape(1), terms)


def body(d_out, router_weight, routes, gate_pre, up_pre):
    group_count = lax.axis_size("expert")
    capacity = gate_pre.shape[0] // group_count
    planes = lax.axis_size("x") * lax.axis_size("y")
    fars = lax.axis_size("far")
    rows, units = gate_pre.shape
    width = d_out.shape[1] // group_count
    block = units // (planes * fars * 2)
    core = lax.axis_index("core")

    outgoing = routed(d_out, router_weight, routes, group_count, capacity)
    place = lax.axis_index(("far", "core"))
    core, place, outgoing = lax.optimization_barrier((core, place, outgoing))
    mine, theirs = hidden_halves(core, gate_pre, up_pre, block)
    incoming = lax.all_to_all(outgoing, "expert", split_axis=0, concat_axis=0, tiled=True)
    incoming = incoming.reshape(rows, width)
    theirs, incoming = lax.optimization_barrier((theirs, incoming))
    met = lax.ppermute(theirs, "core", SWAP)
    incoming_met = lax.ppermute(incoming, "core", SWAP)

    partial = jnp.dot(mine, incoming, preferred_element_type=jnp.float32) + jnp.dot(
        met, incoming_met, preferred_element_type=jnp.float32
    )
    partial = partial.astype(jnp.bfloat16).reshape(planes, fars * block, width)
    partial = lax.all_to_all(partial, ("x", "y"), split_axis=0, concat_axis=0, tiled=True)
    own, passed, sent = summed(place, partial, fars)
    sent = lax.ppermute(sent, ("far", "core"), mirrored(0, fars)).astype(jnp.float32)
    passed = (passed + sent[block:]).astype(jnp.bfloat16)
    passed = lax.ppermute(passed, ("far", "core"), mirrored(1, fars))
    return own + sent[:block] + passed.astype(jnp.float32)


def solution(mesh):
    names = tuple(name for name, _ in GRID)
    sizes = tuple(size for _, size in GRID)
    fine = Mesh(mesh.devices.reshape(sizes + (mesh.shape["expert"],)), names + ("expert",))
    tokens = P(names + ("expert",), None)
    slots = P(names, None)
    return jax.shard_map(
        body,
        mesh=fine,
        in_specs=(tokens, tokens, tokens, slots, slots),
        out_specs=P(names, "expert"),
        check_vma=False,
    )
```

```python
import functools
import itertools

import jax
import jax.numpy as jnp
from jax import lax
from jax.experimental import pallas as pl
from jax.experimental.pallas import tpu as pltpu
from jax.sharding import Mesh, PartitionSpec as P

GRID = (("x", 4), ("y", 4), ("far", 4), ("core", 2))
SWAP = [(0, 1), (1, 0)]
PARTS = 8
PARTNERS = ((1, 3), (3, 1))


def mirrored(step, fars):
    return [
        (2 * far + core, 2 * (far ^ PARTNERS[step][core]) + core)
        for far in range(fars)
        for core in (0, 1)
    ]


def hidden_kernel(block, side, core_ref, gate_ref, up_ref, mine_ref, theirs_ref, gate, up, sems):
    parts, rows, part = gate.shape
    rows_of_plane = mine_ref.shape[0] // (side * side)

    def copies(index):
        columns = pl.ds(index * part, part)
        return (
            pltpu.make_async_copy(gate_ref.at[:, columns], gate.at[index], sems.at[0, index]),
            pltpu.make_async_copy(up_ref.at[:, columns], up.at[index], sems.at[1, index]),
        )

    for index in range(parts):
        for copy in copies(index):
            copy.start()
    core = core_ref[0]
    for index in range(parts):
        for copy in copies(index):
            copy.wait()
        value = gate[index].astype(jnp.float32)
        value = value * (0.5 * jnp.tanh(0.5 * value) + 0.5) * up[index].astype(jnp.float32)
        value = value.astype(jnp.bfloat16).astype(jnp.float32)
        value = value.T.reshape(part // (2 * block), 2, block, rows)
        first = value[:, 0].reshape(part // 2, rows).astype(jnp.bfloat16)
        second = value[:, 1].reshape(part // 2, rows).astype(jnp.bfloat16)
        run = rows_of_plane
        for piece in range(part // 2 // run):
            column, row = divmod(index * (part // 2 // run) + piece, side)
            source = slice(piece * run, (piece + 1) * run)
            where = slice((row * side + column) * run, (row * side + column + 1) * run)

            @pl.when(core == 0)
            def _():
                mine_ref[where, :] = first[source]
                theirs_ref[where, :] = second[source]

            @pl.when(core != 0)
            def _():
                mine_ref[where, :] = second[source]
                theirs_ref[where, :] = first[source]


def hidden_halves(core, gate_pre, up_pre, block, side):
    rows, units = gate_pre.shape
    half = jax.ShapeDtypeStruct((units // 2, rows), jnp.bfloat16)
    buffer = pltpu.VMEM((PARTS, rows, units // PARTS), jnp.bfloat16)
    return pl.pallas_call(
        functools.partial(hidden_kernel, block, side),
        in_specs=[
            pl.BlockSpec(memory_space=pltpu.SMEM),
            pl.BlockSpec(memory_space=pl.ANY),
            pl.BlockSpec(memory_space=pl.ANY),
        ],
        out_specs=[pl.BlockSpec(memory_space=pltpu.VMEM)] * 2,
        out_shape=[half, half],
        scratch_shapes=[buffer, buffer, pltpu.SemaphoreType.DMA((2, PARTS))],
        compiler_params=pltpu.CompilerParams(vmem_limit_bytes=52 << 20),
        cost_estimate=pl.CostEstimate(
            flops=8 * rows * units, bytes_accessed=6 * rows * units, transcendentals=rows * units
        ),
        name="hidden",
    )(core.reshape(1), gate_pre, up_pre)


def routed_kernel(tokens_from, weight_from, routes_from, outgoing_ref, *scratch):
    tokens_ref, weight_ref, routes_ref, sems = scratch
    copies = [
        pltpu.make_async_copy(source, target, sems.at[index])
        for index, (source, target) in enumerate(
            (
                (routes_from, routes_ref),
                (weight_from, weight_ref),
                (tokens_from, tokens_ref),
            )
        )
    ]
    for copy in copies:
        copy.start()
    groups, capacity, width = outgoing_ref.shape
    count = tokens_ref.shape[0]
    earlier = lax.broadcasted_iota(jnp.int32, (count, count), 0)
    later = lax.broadcasted_iota(jnp.int32, (count, count), 1)
    before = (earlier < later).astype(jnp.bfloat16)
    slots = lax.broadcasted_iota(jnp.int32, (capacity, count), 0)
    copies[0].wait()
    copies[1].wait()
    named = routes_ref[...] == 0
    marked = jnp.max(named.astype(jnp.float32), axis=0, keepdims=True)
    weight = jnp.sum(jnp.where(named, weight_ref[...], 0.0), axis=0, keepdims=True)
    position = jnp.dot(
        jnp.broadcast_to(marked, (8, count)).astype(jnp.bfloat16),
        before,
        preferred_element_type=jnp.float32,
    )[:1]
    taken = (slots == position.astype(jnp.int32)) & (marked > 0.5)
    chosen = taken.astype(jnp.bfloat16)
    scale = jnp.sum(jnp.where(taken, weight, 0.0), axis=1, keepdims=True)
    copies[2].wait()
    picked = jnp.dot(chosen, tokens_ref[...], preferred_element_type=jnp.float32)
    picked = (picked * scale).astype(jnp.bfloat16)
    for group in range(groups):
        outgoing_ref[group] = picked[:, group * width : (group + 1) * width]


def routed(tokens, weight, routes, groups, capacity):
    width = tokens.shape[1] // groups
    return pl.pallas_call(
        routed_kernel,
        in_specs=[pl.BlockSpec(memory_space=pl.ANY)] * 3,
        out_specs=pl.BlockSpec(memory_space=pltpu.VMEM),
        out_shape=jax.ShapeDtypeStruct((groups, capacity, width), jnp.bfloat16),
        scratch_shapes=[
            pltpu.VMEM(tokens.shape, tokens.dtype),
            pltpu.VMEM(weight.shape[::-1], weight.dtype),
            pltpu.VMEM(routes.shape[::-1], routes.dtype),
            pltpu.SemaphoreType.DMA((3,)),
        ],
        compiler_params=pltpu.CompilerParams(vmem_limit_bytes=62 << 20),
        name="routed",
    )(tokens, weight.T, routes.T)


def sum_kernel(place_ref, terms_ref, own_ref, passed_ref, sent_ref):
    block, width = own_ref.shape
    total = terms_ref[0].astype(jnp.float32)
    for index in range(1, terms_ref.shape[0]):
        total = total + terms_ref[index].astype(jnp.float32)
    total = total.reshape(-1, block, width)
    for place, (far, core) in enumerate(itertools.product(range(total.shape[0]), (0, 1))):

        @pl.when(place_ref[0] == place)
        def _():
            own_ref[...] = total[far]
            passed_ref[...] = total[far ^ PARTNERS[1][core]]
            sent = jnp.concatenate([total[far ^ PARTNERS[0][core]], total[far ^ 2]], axis=0)
            sent_ref[...] = sent.astype(jnp.bfloat16)


def summed(place, terms, fars):
    block, width = terms.shape[1] // fars, terms.shape[2]
    piece = jax.ShapeDtypeStruct((block, width), jnp.float32)
    return pl.pallas_call(
        sum_kernel,
        in_specs=[
            pl.BlockSpec(memory_space=pltpu.SMEM),
            pl.BlockSpec(memory_space=pltpu.VMEM),
        ],
        out_specs=[pl.BlockSpec(memory_space=pltpu.VMEM)] * 3,
        out_shape=[piece, piece, jax.ShapeDtypeStruct((2 * block, width), jnp.bfloat16)],
        compiler_params=pltpu.CompilerParams(vmem_limit_bytes=16 << 20),
        name="plane_sum",
    )(place.reshape(1), terms)


def body(d_out, router_weight, routes, gate_pre, up_pre):
    group_count = lax.axis_size("expert")
    capacity = gate_pre.shape[0] // group_count
    planes = lax.axis_size("x") * lax.axis_size("y")
    fars = lax.axis_size("far")
    rows, units = gate_pre.shape
    width = d_out.shape[1] // group_count
    block = units // (planes * fars * 2)
    core = lax.axis_index("core")

    outgoing = routed(d_out, router_weight, routes, group_count, capacity)
    place = lax.axis_index(("far", "core"))
    core, place, outgoing = lax.optimization_barrier((core, place, outgoing))
    mine, theirs = hidden_halves(core, gate_pre, up_pre, block, lax.axis_size("x"))
    incoming = lax.all_to_all(outgoing, "expert", split_axis=0, concat_axis=0, tiled=True)
    incoming = incoming.reshape(rows, width)
    theirs, incoming = lax.optimization_barrier((theirs, incoming))
    met = lax.ppermute(theirs, "core", SWAP)
    incoming_met = lax.ppermute(incoming, "core", SWAP)

    partial = jnp.dot(mine, incoming, preferred_element_type=jnp.float32) + jnp.dot(
        met, incoming_met, preferred_element_type=jnp.float32
    )
    partial = partial.astype(jnp.bfloat16).reshape(planes, fars * block, width)
    partial = lax.all_to_all(partial, ("y", "x"), split_axis=0, concat_axis=0, tiled=True)
    own, passed, sent = summed(place, partial, fars)
    sent = lax.ppermute(sent, ("far", "core"), mirrored(0, fars)).astype(jnp.float32)
    passed = (passed + sent[block:]).astype(jnp.bfloat16)
    passed = lax.ppermute(passed, ("far", "core"), mirrored(1, fars))
    return own + sent[:block] + passed.astype(jnp.float32)


def solution(mesh):
    names = tuple(name for name, _ in GRID)
    sizes = tuple(size for _, size in GRID)
    fine = Mesh(mesh.devices.reshape(sizes + (mesh.shape["expert"],)), names + ("expert",))
    tokens = P(names + ("expert",), None)
    slots = P(names, None)
    return jax.shard_map(
        body,
        mesh=fine,
        in_specs=(tokens, tokens, tokens, slots, slots),
        out_specs=P(names, "expert"),
        check_vma=False,
    )
```
